32 devices in a mesh: section: 4 (over x, core), feat: 8 (over z, y).
Axes of the slice: x: 2, y: 2, z: 4, core: 2. Of those that a mesh axis runs over, the one named last changes fastest.
Arguments:
- residual: bfloat16 [4, 128, 4096], P('section'), may hold values from -6 to 6
- enc_weight: bfloat16 [4, 4096, 16384], P('section', None, 'feat'), may hold values from -0.09375 to 0.09375
- dec_weight: bfloat16 [4, 16384, 4, 4096], P('section', 'feat'), may hold values from -1 to 1
- latent_ids: int32 [4, 128, 64], P('section'), may hold values from 0 to 16383, all different within a row
Outputs:
- written: bfloat16 [4, 4096, 128], P('section', 'feat')
The draws below stay inside these ranges and needn't reach their ends.
Inputs may be any that keep to these rules, and one draw needn't show every extreme that they name: Each row latent_ids[l, n, :] names 64 different latents.
All inputs are finite; a program needn't handle non-finite values.
Results may differ from the reference program's by a relative error of at most 0.0049.
Values may be sent and summed in bfloat16 or wider, within the bound.
No kernel may reach another device: no remote copies, remote signals or barrier semaphores. Data moves between devices by JAX's collectives and lax.ppermute only.
A program may use at most 192 MiB of HBM per device.

```python
import jax
import jax.numpy as jnp
from jax import lax

D = 4096
F = 16384
K = 64
TOK = 128
L = 4


def spiked(values, own_key, source, target, parts, factor):
    owner, partner = [(jnp.arange(values.shape[position]) // (values.shape[position] // parts)).reshape([-1 if axis == position else 1 for axis in range(values.ndim)]) for position in (source, target)]
    chosen = jax.random.permutation(own_key, parts)[partner]
    strong = (owner == chosen) | (owner == (partner + parts // 2) % parts)
    return jnp.where(strong, factor * values, values)


def shard_levels(stream_key, dims, cuts, low, high):
    def one(dim, shards_of):
        heights = jax.random.uniform(jax.random.fold_in(jax.random.fold_in(stream_key, 6), dim), (shards_of,), jnp.float32, low / len(cuts), high / len(cuts))
        return jnp.repeat(jnp.exp(heights), dims[dim] // shards_of).reshape((-1,) + (1,) * (len(dims) - dim - 1))

    gain = one(*cuts[0])
    for cut in cuts[1:]:
        gain = gain * one(*cut)
    return gain


def different_ones(rng, rows, count, top, lift):
    ranking = jax.random.permutation(jax.random.fold_in(rng, 1), count)
    favour = ranking
    for power in range(3):
        favour = favour * favour // count
    favour = favour * lift // count
    lots = jax.random.randint(jax.random.fold_in(rng, 2), (rows, count), 0, 4096) + favour
    holders = jax.random.permutation(jax.random.fold_in(rng, 3), rows)[jnp.arange(count) % rows]
    lots = jnp.where(jnp.arange(rows)[:, None] == holders[None, :], 1 << 14, lots)
    merit = lots * count + jnp.arange(count)
    return lax.top_k(merit.astype(jnp.int32), top)[1].astype(jnp.int32)


def bell_draw(rng, extent, width, most, split=(), held_as=jnp.bfloat16):
    factor_of = shard_levels(rng, extent, split, -0.22, 0.18) if split else 1.0
    drawn = jax.random.normal(rng, extent, jnp.float32) * width * factor_of
    return jnp.minimum(jnp.maximum(drawn, -most), most).astype(held_as)


def heavy_noise(rng, extent, scale, reach, pieces, heavy, dtype=jnp.bfloat16):
    array = scale * jax.random.normal(rng, extent, jnp.float32)
    if pieces:
        array = array * shard_levels(rng, extent, pieces, -0.22, 0.18)
    return jnp.clip(spiked(array, jax.random.fold_in(rng, 3), *heavy), -reach, reach).astype(dtype)


def setup_inputs(seed: int = 0) -> dict:
    key_of = jax.random.split(jax.random.key(seed), 5)
    residual = bell_draw(key_of[0], (L, TOK, D), 1.0, 6.0, ((0, 4),))
    enc_weight = bell_draw(key_of[1], (L, D, F), D ** -0.5, 0.09375, ((0, 4), (2, 8)))
    dec_weight = heavy_noise(key_of[2], (L, F, L, D), K ** -0.5, 1.0, ((0, 4), (1, 8)), (1, 3, 8, 2.0))
    latent_ids = different_ones(key_of[3], L * TOK, F, K, 32).reshape((L, TOK, K))
    return {"residual": residual, "enc_weight": enc_weight, "dec_weight": dec_weight, "latent_ids": latent_ids}


def reference(residual, enc_weight, dec_weight, latent_ids):
    layers = residual.shape[0]
    totals = [jnp.zeros((TOK, D), jnp.float32) for target in range(layers)]
    for source in range(layers):
        ids_here = latent_ids[source]
        enc_cols = jnp.take(enc_weight[source], ids_here, axis=1)
        pre_acts = jnp.einsum("nd,dnk->nk", residual[source].astype(jnp.float32), enc_cols.astype(jnp.float32))
        latent_vals = jnp.maximum(pre_acts, 0.0).astype(jnp.bfloat16)
        for target in range(source, layers):
            dec_rows = jnp.take(dec_weight[source, :, target, :], ids_here, axis=0)
            contrib = jnp.einsum("nk,nkd->nd", latent_vals.astype(jnp.float32), dec_rows.astype(jnp.float32))
            totals[target] = totals[target] + contrib
    return jnp.stack([block.T for block in totals]).astype(jnp.bfloat16)
```

```python
import functools

import jax
import jax.numpy as jnp
from jax import lax
from jax.experimental import pallas as pl
from jax.experimental.pallas import tpu as pltpu
from jax.sharding import PartitionSpec as P

LANES = 128
GROUP = 4
RING = 2
WIDE = 4
ENC_SLOTS = 4
F32 = jnp.float32
BF16 = jnp.bfloat16


def iota(shape, dim):
    return lax.broadcasted_iota(jnp.int32, shape, dim)


def dot(a, b):
    return jnp.dot(a, b, preferred_element_type=F32)


def dot_t(a, b):
    return lax.dot_general(a, b, (((1,), (1,)), ((), ())), preferred_element_type=F32)


def kernel(
    feats,
    relative,
    pos_ref,
    ids_hbm,
    res_hbm,
    enc_hbm,
    dec_hbm,
    out_hbm,
    ids_v,
    lo_v,
    sh_v,
    res_v,
    enc_v,
    list_v,
    list_s,
    pre_v,
    acts_v,
    lhs_v,
    buf,
    acc,
    out_v,
    small_sem,
    enc_sem,
    dec_sem,
    out_sem,
):
    tokens, width = res_v.shape
    shard = acts_v.shape[1]
    slots = list_v.shape[1]
    rows_hi = shard // LANES
    max_blocks = slots // LANES
    wides = out_v.shape[1]
    section_pos, feat_pos = pos_ref[0], pos_ref[1]
    core = section_pos % 2

    ids_copy = pltpu.make_async_copy(ids_hbm, ids_v, small_sem.at[0])
    ids_copy.start()
    res_copy = pltpu.make_async_copy(res_hbm, res_v, small_sem.at[1])
    res_copy.start()
    depth = enc_v.shape[1]
    enc_steps = width // depth

    def enc_copy(step):
        return pltpu.make_async_copy(
            enc_hbm.at[pl.ds(step * depth, depth)], enc_v.at[step % ENC_SLOTS], enc_sem.at[step % ENC_SLOTS]
        )

    for step in range(min(ENC_SLOTS, enc_steps)):
        enc_copy(step).start()

    ids_copy.wait()
    local = ids_v[...] - feat_pos * shard
    inside = (local >= 0) & (local < shard)
    lo_v[...] = jnp.where(inside, local & (LANES - 1), -1)
    sh_v[...] = jnp.where(inside, jnp.left_shift(1, (local >> 7) & 31), 0)
    lane_of = iota((LANES, tokens), 0)

    def gather_bits(k, bits):
        hit = lo_v[pl.ds(k, 1), :] == lane_of
        return bits | jnp.where(hit, sh_v[pl.ds(k, 1), :], 0)

    bits_t = lax.fori_loop(0, ids_v.shape[0], gather_bits, jnp.zeros((LANES, tokens), jnp.int32), unroll=8)
    bits = bits_t.T
    union = bits
    while union.shape[0] > 1:
        half = union.shape[0] // 2
        union = union[:half] | union[half:]

    hi_of = iota((LANES, LANES), 0)
    lane = iota((LANES, LANES), 1)
    flags = jnp.where(hi_of < rows_hi, jnp.right_shift(jnp.broadcast_to(union, (LANES, LANES)), hi_of & 31) & 1, 0)
    flags_f = flags.astype(F32)
    flags_b = flags_f.astype(BF16)
    upper = (hi_of <= lane).astype(F32).astype(BF16)
    inclusive = dot(flags_b, upper)
    row_total = jnp.sum(flags_f, axis=1, keepdims=True)
    below = (lane < hi_of).astype(F32).astype(BF16)
    row_start = dot(below, jnp.broadcast_to(row_total, (LANES, LANES)).astype(BF16))
    row_end = row_start + row_total
    count = jnp.sum(flags_f).astype(jnp.int32)
    rank = jnp.where(flags > 0, row_start + inclusive - 1.0, -1.0)

    slot = iota((LANES, slots), 1).astype(F32)
    start_w = jnp.concatenate([row_start] * max_blocks, axis=1)
    end_w = jnp.concatenate([row_end] * max_blocks, axis=1)
    in_row = (start_w <= slot) & (slot < end_w)
    in_row_f = in_row.astype(F32)
    row_of = jnp.sum(in_row_f * iota((LANES, slots), 0).astype(F32), axis=0, keepdims=True)
    place = jnp.sum(jnp.where(in_row, slot - start_w, 0.0), axis=0, keepdims=True)
    prefix = dot(inclusive.T.astype(BF16), in_row_f.astype(BF16))
    lane_in = jnp.sum((prefix <= place).astype(F32), axis=0, keepdims=True)
    latent = row_of * float(LANES) + lane_in
    latent = jnp.where(iota((1, slots), 1) < count, latent, 0.0).astype(jnp.int32)
    list_v[...] = latent
    list_copy = pltpu.make_async_copy(list_v, list_s, small_sem.at[2])
    list_copy.start()
    blocks = jnp.maximum(1, (count + (LANES - 1)) // LANES)
    groups = (blocks + (GROUP - 1)) // GROUP

    def issue(group):
        ring = lax.rem(group, RING)
        here = jnp.minimum(GROUP, blocks - group * GROUP)

        def block(b, carry):
            place = ring * GROUP + b
            base = (group * GROUP + b) * LANES

            def row(i, carry):
                latent_id = list_s[0, base + i]
                pltpu.make_async_copy(
                    dec_hbm.at[latent_id],
                    buf.at[place, :, :, pl.ds(pl.multiple_of(2 * i, 2), 2), :],
                    dec_sem.at[place],
                ).start()
                return carry

            return lax.fori_loop(0, LANES, row, carry, unroll=8)

        lax.fori_loop(0, here, block, 0)

    def encode(step):
        enc_copy(step).wait()
        part = dot(res_v[:, pl.ds(step * depth, depth)], enc_v[step % ENC_SLOTS])
        if step == 0:
            pre_v[...] = part
        else:
            pre_v[...] += part
        if step + ENC_SLOTS < enc_steps:
            enc_copy(step + ENC_SLOTS).start()

    res_copy.wait()
    early = min(2, enc_steps)
    for step in range(early):
        encode(step)
    list_copy.wait()
    issue(0)
    for step in range(early, enc_steps):
        encode(step)

    for hi in range(rows_hi):
        columns = slice(hi * LANES, (hi + 1) * LANES)
        active = (jnp.right_shift(bits, hi) & 1) > 0
        acts_v[:, columns] = jnp.where(active, jnp.maximum(pre_v[:, columns], 0.0), 0.0).astype(BF16)

    @pl.when(groups > 1)
    def _():
        issue(1)

    twice = ((iota((LANES, 2 * LANES), 1) >> 1) == iota((LANES, 2 * LANES), 0)).astype(F32).astype(BF16)
    parity = iota((tokens, 2 * LANES), 1) & 1

    def compact(b, carry):
        want = (iota((LANES, LANES), 0) + b * LANES).astype(F32)
        chosen = jnp.concatenate(
            [(rank[hi : hi + 1, :] == want).astype(F32).astype(BF16) for hi in range(rows_hi)], axis=1
        )
        picked = dot_t(acts_v[...], chosen).astype(BF16)
        doubled = dot(picked, twice)
        lhs_v[b, :tokens, :] = jnp.where(parity == core, doubled, 0.0).astype(BF16)
        lhs_v[b, tokens:, :] = jnp.where(parity == core, 0.0, doubled).astype(BF16)
        return carry

    lax.fori_loop(0, blocks, compact, 0)

    def out_copy(pair, wide, dest):
        return pltpu.make_async_copy(out_v.at[pair, wide], out_hbm.at[:, pair, dest], out_sem)

    def multiply(group, size, first, last):
        ring = lax.rem(group, RING)
        for b in range(size):
            place = ring * GROUP + b
            pltpu.make_async_copy(buf.at[place], buf.at[place], dec_sem.at[place]).wait()
        left = jnp.concatenate([lhs_v[group * GROUP + b] for b in range(size)], axis=1)

        def wide_step(i, carry):
            pair = i // wides
            wide = lax.rem(i, wides)
            right = jnp.concatenate(
                [
                    jnp.concatenate([buf[ring * GROUP + b, wide * WIDE + q, pair] for q in range(WIDE)], axis=1)
                    for b in range(size)
                ],
                axis=0,
            )
            total = dot(left, right)
            if not first:
                total = total + acc[pair, wide]
            if last:
                narrow = total.astype(BF16)
                for part in range(2):
                    for q in range(WIDE):
                        out_v[pair, wide, part, q] = narrow[
                            part * tokens : (part + 1) * tokens, q * LANES : (q + 1) * LANES
                        ]
                if relative:
                    apart = jnp.bitwise_xor(wide, feat_pos)
                    dest = (apart & 1) * (feats // 2) + (apart >> 1)
                else:
                    dest = wide
                out_copy(pair, wide, dest).start()
            else:
                acc[pair, wide] = total
            return carry

        lax.fori_loop(0, 2 * wides, wide_step, 0)

    def each_group(group, carry):
        here = blocks - group * GROUP
        for first in (True, False):
            at = (group == 0) if first else (group > 0)
            if max_blocks > GROUP:

                @pl.when(at & (here > GROUP))
                def _():
                    multiply(group, GROUP, first, False)

            elif not first:
                continue
            for size in range(1, min(GROUP, max_blocks) + 1):

                @pl.when(at & (here == size))
                def _():
                    multiply(group, size, first, True)

        if max_blocks > RING * GROUP:

            @pl.when(group + RING < groups)
            def _():
                issue(group + RING)

        return carry

    lax.fori_loop(0, groups, each_group, 0)
    for pair in range(2):
        for wide in range(wides):
            out_copy(pair, wide, 0).wait()


def partial_sums(position, ids, residual, enc, dec, feats, relative):
    tokens, width = residual.shape
    shard = enc.shape[1]
    tiles = width // LANES
    wides = tiles // WIDE
    max_blocks = -(-shard // LANES)
    slots = max_blocks * LANES
    depth = min(512, width)
    return pl.pallas_call(
        functools.partial(kernel, feats, relative),
        out_shape=jax.ShapeDtypeStruct((2, 2, wides, WIDE, tokens, LANES), BF16),
        in_specs=[pl.BlockSpec(memory_space=pltpu.SMEM)] + [pl.BlockSpec(memory_space=pl.ANY)] * 4,
        out_specs=pl.BlockSpec(memory_space=pl.ANY),
        scratch_shapes=[
            pltpu.VMEM(ids.shape, jnp.int32),
            pltpu.VMEM(ids.shape, jnp.int32),
            pltpu.VMEM(ids.shape, jnp.int32),
            pltpu.VMEM((tokens, width), BF16),
            pltpu.VMEM((ENC_SLOTS, depth, shard), BF16),
            pltpu.VMEM((1, slots), jnp.int32),
            pltpu.SMEM((1, slots), jnp.int32),
            pltpu.VMEM((tokens, shard), F32),
            pltpu.VMEM((tokens, shard), BF16),
            pltpu.VMEM((max_blocks, 2 * tokens, 2 * LANES), BF16),
            pltpu.VMEM((min(RING * GROUP, max_blocks), tiles, 2, 2 * LANES, LANES), BF16),
            pltpu.VMEM((2, wides, 2 * tokens, WIDE * LANES), F32),
            pltpu.VMEM((2, wides, 2, WIDE, tokens, LANES), BF16),
            pltpu.SemaphoreType.DMA((3,)),
            pltpu.SemaphoreType.DMA((ENC_SLOTS,)),
            pltpu.SemaphoreType.DMA((RING * GROUP,)),
            pltpu.SemaphoreType.DMA,
        ],
        compiler_params=pltpu.CompilerParams(vmem_limit_bytes=62 * 2**20),
        cost_estimate=pl.CostEstimate(
            flops=4 * tokens * width * shard, bytes_accessed=2 * width * shard * 3, transcendentals=0
        ),
    )(position, ids, residual, enc, dec)


def local(residual, enc_weight, dec_weight, latent_ids):
    feats = lax.axis_size("feat")
    section_pos = lax.axis_index("section")
    feat_pos = lax.axis_index("feat")
    tokens, width = residual.shape[1:]
    shard = enc_weight.shape[2]
    tiles = width // LANES
    own = width // feats
    relative = own == WIDE * LANES
    position = jnp.stack([section_pos, feat_pos]).astype(jnp.int32)
    ids = latent_ids[0].T
    dec = dec_weight[0].reshape(shard, 2, 2, tiles, LANES).transpose(0, 3, 1, 2, 4)
    sums = partial_sums(position, ids, residual[0], enc_weight[0], dec, feats, relative)
    if relative:
        blocks = sums.reshape(2, 2, 2, feats // 2, WIDE, tokens, LANES)
    else:
        blocks = jnp.transpose(sums, (0, 1, 2, 3, 5, 4)).reshape(2, 2, feats, own, tokens)
        apart = jnp.arange(feats)
        apart = (apart % (feats // 2)) * 2 + apart // (feats // 2)
        blocks = jnp.take(blocks, apart ^ feat_pos, axis=2).reshape(2, 2, 2, feats // 2, own, tokens)
    keep, send = blocks[0], blocks[1]

    def across_feat(x, bit, sections):
        pairs = [(s * feats + f, s * feats + (f ^ bit)) for s in sections for f in range(feats)]
        return lax.ppermute(x, ("section", "feat"), pairs)

    def reduce_feat(x, sections):
        x = x.astype(F32)
        half = x[0] + across_feat(x[1].astype(BF16), 1, sections).astype(F32)
        narrow = half.astype(BF16)
        total = half[0]
        for device in range(1, feats // 2):
            total = total + across_feat(narrow[device], 2 * device, sections).astype(F32)
        return total

    late = keep[1].astype(F32) + lax.ppermute(send[1], "section", [(0, 1), (1, 0), (2, 3)]).astype(F32)
    early = keep[0].astype(F32) + lax.ppermute(send[0], "section", [(0, 1)]).astype(F32)
    late = reduce_feat(late, (0, 1, 2, 3))
    early = reduce_feat(early, (0, 1))
    carried = lax.ppermute(late, "section", [(0, 2), (1, 3)])
    written = jnp.where(section_pos < 2, early, late + carried)
    if relative:
        written = jnp.transpose(written, (0, 2, 1)).reshape(own, tokens)
    return written.astype(BF16)[None]


def solution(mesh):
    in_specs = (
        P("section", None, None),
        P("section", None, "feat"),
        P("section", "feat", None, None),
        P("section", None, None),
    )
    out_specs = P("section", "feat", None)
    return jax.shard_map(local, mesh=mesh, in_specs=in_specs, out_specs=out_specs, check_vma=False)
```

```python
import functools

import jax
import jax.numpy as jnp
from jax import lax
from jax.experimental import pallas as pl
from jax.experimental.pallas import tpu as pltpu
from jax.sharding import PartitionSpec as P

LANES = 128
GROUP = 4
RING = 7
WIDE = 4
LEAD = 2
WINDOW = 5
F32 = jnp.float32
BF16 = jnp.bfloat16


def iota(shape, dim):
    return lax.broadcasted_iota(jnp.int32, shape, dim)


def dot(a, b):
    return jnp.dot(a, b, preferred_element_type=F32)


def dot_t(a, b):
    return lax.dot_general(a, b, (((1,), (1,)), ((), ())), preferred_element_type=F32)


def kernel(
    feats,
    relative,
    pos_ref,
    ids_hbm,
    res_hbm,
    enc_hbm,
    dec_hbm,
    keep_early,
    send_early,
    keep_late,
    send_late,
    ids_v,
    lo_v,
    sh_v,
    bits_v,
    rank_v,
    res_v,
    enc_v,
    list_v,
    list_s,
    acts_v,
    lhs_v,
    buf,
    acc,
    out_v,
    small_sem,
    enc_sem,
    dec_sem,
    out_sem,
):
    tokens, width = res_v.shape
    shard = acts_v.shape[1]
    slots = list_v.shape[1]
    rows_hi = shard // LANES
    max_blocks = slots // LANES
    ring = buf.shape[0]
    wides = acc.shape[1]
    section_pos, feat_pos = pos_ref[0], pos_ref[1]
    core = section_pos % 2

    ids_copy = pltpu.make_async_copy(ids_hbm, ids_v, small_sem.at[0])
    ids_copy.start()
    res_copy = pltpu.make_async_copy(res_hbm, res_v, small_sem.at[1])
    res_copy.start()
    chunk = min(4 * LANES, shard)
    chunks = shard // chunk

    def enc_copy(i):
        columns = pl.ds(i * chunk, chunk) if isinstance(i, int) else pl.ds(pl.multiple_of(i * chunk, chunk), chunk)
        return pltpu.make_async_copy(enc_hbm.at[:, columns], enc_v.at[i], enc_sem.at[i])

    early = (chunks + 1) // 2
    for i in range(early):
        enc_copy(i).start()

    ids_copy.wait()
    local = ids_v[...] - feat_pos * shard
    inside = (local >= 0) & (local < shard)
    lo_v[...] = jnp.where(inside, local & (LANES - 1), -1)
    sh_v[...] = jnp.where(inside, jnp.left_shift(1, (local >> 7) & 31), 0)
    lane_of = iota((LANES, tokens), 0)

    def gather_bits(k, bits):
        hit = lo_v[pl.ds(k, 1), :] == lane_of
        return bits | jnp.where(hit, sh_v[pl.ds(k, 1), :], 0)

    bits_t = lax.fori_loop(0, ids_v.shape[0], gather_bits, jnp.zeros((LANES, tokens), jnp.int32), unroll=8)
    bits = bits_t.T
    bits_v[...] = bits
    union = bits
    while union.shape[0] > 1:
        half = union.shape[0] // 2
        union = union[:half] | union[half:]

    rows = 16 * (-(-rows_hi // 16))
    hi_of = iota((rows, LANES), 0)
    flags = jnp.where(hi_of < rows_hi, jnp.right_shift(jnp.broadcast_to(union, (rows, LANES)), hi_of & 31) & 1, 0)
    flags_f = flags.astype(F32)
    upper = (iota((LANES, LANES), 0) <= iota((LANES, LANES), 1)).astype(F32).astype(BF16)
    inclusive = dot(flags_f.astype(BF16), upper)
    row_total = jnp.broadcast_to(jnp.sum(flags_f, axis=1, keepdims=True), (rows, LANES))
    below = (iota((rows, rows), 1) < iota((rows, rows), 0)).astype(F32).astype(BF16)
    row_start = dot(below, row_total.astype(BF16))
    row_end = row_start + row_total
    count = jnp.sum(flags_f).astype(jnp.int32)
    rank_v[...] = jnp.where(flags > 0, row_start + inclusive - 1.0, -1.0)

    slot = iota((rows, slots), 1).astype(F32)
    start_w = jnp.concatenate([row_start] * max_blocks, axis=1)
    end_w = jnp.concatenate([row_end] * max_blocks, axis=1)
    in_row = (start_w <= slot) & (slot < end_w)
    in_row_f = in_row.astype(F32)
    row_of = jnp.sum(in_row_f * iota((rows, slots), 0).astype(F32), axis=0, keepdims=True)
    place = jnp.sum(jnp.where(in_row, slot - start_w, 0.0), axis=0, keepdims=True)
    tall = jnp.concatenate([inclusive, jnp.zeros((LANES - rows, LANES), F32)], axis=0) if rows < LANES else inclusive
    prefix = dot(tall.T[:, :rows].astype(BF16), in_row_f.astype(BF16))
    lane_in = jnp.sum((prefix <= place).astype(F32), axis=0, keepdims=True)
    latent = row_of * float(LANES) + lane_in
    slot_row = iota((1, slots), 1)
    list_v[...] = jnp.where(slot_row < count, latent.astype(jnp.int32), slot_row)
    list_copy = pltpu.make_async_copy(list_v, list_s, small_sem.at[2])
    list_copy.start()
    blocks = jnp.maximum(1, (count + (LANES - 1)) // LANES)
    groups = (blocks + (GROUP - 1)) // GROUP

    def gather(place, base, i):
        pltpu.make_async_copy(
            dec_hbm.at[list_s[0, base + i]],
            buf.at[place, :, :, pl.ds(pl.multiple_of(2 * i, 2), 2), :],
            dec_sem.at[place],
        ).start()

    def issue(block, carry):
        place = lax.rem(block, ring)

        def row(i, carry):
            gather(place, block * LANES, i)
            return carry

        return lax.fori_loop(0, LANES, row, carry, unroll=True)

    def encode(i):
        enc_copy(i).wait()
        pre = dot(res_v[...], enc_v[i])
        for q in range(chunk // LANES):
            hi = i * (chunk // LANES) + q
            active = (jnp.right_shift(bits_v[...], hi) & 1) > 0
            piece = jnp.maximum(pre[:, q * LANES : (q + 1) * LANES], 0.0)
            acts_v[:, pl.ds(pl.multiple_of(hi * LANES, LANES), LANES)] = jnp.where(active, piece, 0.0).astype(BF16)

    def encode_step(i, carry):
        encode(i)
        return carry

    res_copy.wait()
    for i in range(early, chunks):
        enc_copy(i).start()
    first_blocks = jnp.minimum(blocks, ring)
    lead = jnp.minimum(blocks, LEAD)
    lax.fori_loop(0, early, encode_step, 0)
    list_copy.wait()
    lax.fori_loop(0, lead, issue, 0)
    lax.fori_loop(early, chunks, encode_step, 0)
    lax.fori_loop(lead, first_blocks, issue, 0)

    twice = ((iota((LANES, 2 * LANES), 1) >> 1) == iota((LANES, 2 * LANES), 0)).astype(F32).astype(BF16)
    parity = iota((tokens, 2 * LANES), 1) & 1
    window = min(WINDOW, rows_hi)

    def row_at(slot):
        return list_s[0, jnp.clip(slot, 0, jnp.maximum(count - 1, 0))] >> 7

    def compact(b, start, many):
        want = (iota((LANES, LANES), 0) + b * LANES).astype(F32)
        chosen = jnp.concatenate(
            [(rank_v[pl.ds(start + q, 1), :] == want).astype(F32).astype(BF16) for q in range(many)], axis=1
        )
        from_acts = acts_v[:, pl.ds(pl.multiple_of(start * LANES, LANES), many * LANES)]
        picked = dot_t(from_acts, chosen).astype(BF16)
        doubled = dot(picked, twice)
        lhs_v[b, :tokens, :] = jnp.where(parity == core, doubled, 0.0).astype(BF16)
        lhs_v[b, tokens:, :] = jnp.where(parity == core, 0.0, doubled).astype(BF16)

    def compact_wide(b, carry):
        compact(b, 0, rows_hi)
        return carry

    starts = [jnp.minimum(row_at(b * LANES), rows_hi - window) for b in range(ring)]
    narrow_fits = blocks >= ring
    for b in range(ring):
        narrow_fits = narrow_fits & (row_at(b * LANES + LANES - 1) < starts[b] + window)

    @pl.when(narrow_fits)
    def _():
        for b in range(ring):
            compact(b, starts[b], window)

    lax.fori_loop(jnp.where(narrow_fits, ring, 0), blocks, compact_wide, 0)

    outs = {(0, 0): keep_early, (0, 1): send_early, (1, 0): keep_late, (1, 1): send_late}

    def out_copy(pair, part, wide, dest):
        return pltpu.make_async_copy(out_v.at[pair, wide, part], outs[pair, part].at[dest], out_sem)

    def multiply(group, size, first, last):
        places = [lax.rem(group * GROUP + b, ring) for b in range(size)]
        for place in places:
            pltpu.make_async_copy(buf.at[place], buf.at[place], dec_sem.at[place]).wait()
        left = jnp.concatenate([lhs_v[group * GROUP + b] for b in range(size)], axis=1)
        for pair in (1, 0):

            def wide_step(wide, carry):
                right = jnp.concatenate(
                    [
                        jnp.concatenate([buf[place, wide * WIDE + q, pair] for q in range(WIDE)], axis=1)
                        for place in places
                    ],
                    axis=0,
                )
                total = dot(left, right)
                if not first:
                    total = total + acc[pair, wide]
                if last:
                    narrow = total.astype(BF16)
                    for part in range(2):
                        for q in range(WIDE):
                            out_v[pair, wide, part, q] = narrow[
                                part * tokens : (part + 1) * tokens, q * LANES : (q + 1) * LANES
                            ]
                else:
                    acc[pair, wide] = total
                return carry

            lax.fori_loop(0, wides, wide_step, 0, unroll=True)
            if last:
                for wide in range(wides):
                    if relative:
                        apart = jnp.bitwise_xor(wide, feat_pos)
                        dest = (apart & 1) * (feats // 2) + (apart >> 1)
                    else:
                        dest = wide
                    for part in range(2):
                        out_copy(pair, part, wide, dest).start()

    def each_group(group, carry):
        here = blocks - group * GROUP
        for first in (True, False):
            at = (group == 0) if first else (group > 0)
            if max_blocks > GROUP:

                @pl.when(at & (here > GROUP))
                def _():
                    multiply(group, GROUP, first, False)

            elif not first:
                continue
            for size in range(1, min(GROUP, max_blocks) + 1):

                @pl.when(at & (here == size))
                def _():
                    multiply(group, size, first, True)

        if max_blocks > ring:
            done = (group + 1) * GROUP
            lax.fori_loop(jnp.minimum(blocks, done - GROUP + ring), jnp.minimum(blocks, done + ring), issue, 0)

        return carry

    lax.fori_loop(0, groups, each_group, 0)
    for pair in range(2):
        for wide in range(wides):
            for part in range(2):
                out_copy(pair, part, wide, 0).wait()


def partial_sums(position, ids, residual, enc, dec, feats, relative):
    tokens, width = residual.shape
    shard = enc.shape[1]
    tiles = width // LANES
    wides = tiles // WIDE
    max_blocks = -(-shard // LANES)
    slots = max_blocks * LANES
    ring = min(RING, max_blocks)
    rows = 16 * (-(-max_blocks // 16))
    chunks = shard // min(4 * LANES, shard)
    return pl.pallas_call(
        functools.partial(kernel, feats, relative),
        out_shape=[jax.ShapeDtypeStruct((wides, WIDE, tokens, LANES), BF16)] * 4,
        in_specs=[pl.BlockSpec(memory_space=pltpu.SMEM)] + [pl.BlockSpec(memory_space=pl.ANY)] * 4,
        out_specs=[pl.BlockSpec(memory_space=pl.ANY)] * 4,
        scratch_shapes=[
            pltpu.VMEM(ids.shape, jnp.int32),
            pltpu.VMEM(ids.shape, jnp.int32),
            pltpu.VMEM(ids.shape, jnp.int32),
            pltpu.VMEM((tokens, LANES), jnp.int32),
            pltpu.VMEM((rows, LANES), F32),
            pltpu.VMEM((tokens, width), BF16),
            pltpu.VMEM((chunks, width, shard // chunks), BF16),
            pltpu.VMEM((1, slots), jnp.int32),
            pltpu.SMEM((1, slots), jnp.int32),
            pltpu.VMEM((tokens, shard), BF16),
            pltpu.VMEM((max_blocks, 2 * tokens, 2 * LANES), BF16),
            pltpu.VMEM((ring, tiles, 2, 2 * LANES, LANES), BF16),
            pltpu.VMEM((2, wides, 2 * tokens, WIDE * LANES), F32),
            pltpu.VMEM((2, wides, 2, WIDE, tokens, LANES), BF16),
            pltpu.SemaphoreType.DMA((3,)),
            pltpu.SemaphoreType.DMA((chunks,)),
            pltpu.SemaphoreType.DMA((ring,)),
            pltpu.SemaphoreType.DMA,
        ],
        compiler_params=pltpu.CompilerParams(vmem_limit_bytes=62 * 2**20),
        cost_estimate=pl.CostEstimate(
            flops=4 * tokens * width * shard, bytes_accessed=2 * width * shard * 3, transcendentals=0
        ),
    )(position, ids, residual, enc, dec)


def local(residual, enc_weight, dec_weight, latent_ids):
    feats = lax.axis_size("feat")
    section_pos = lax.axis_index("section")
    feat_pos = lax.axis_index("feat")
    tokens, width = residual.shape[1:]
    shard = enc_weight.shape[2]
    tiles = width // LANES
    own = width // feats
    relative = own == WIDE * LANES
    position = jnp.stack([section_pos, feat_pos]).astype(jnp.int32)
    ids = latent_ids[0].T
    dec = dec_weight[0].reshape(shard, 2, 2, tiles, LANES).transpose(0, 3, 1, 2, 4)
    sums = partial_sums(position, ids, residual[0], enc_weight[0], dec, feats, relative)

    def blocks_of(part):
        if relative:
            return part.reshape(2, feats // 2, own, LANES)
        part = jnp.transpose(part, (0, 1, 3, 2)).reshape(feats, own, tokens)
        apart = jnp.arange(feats)
        apart = (apart % (feats // 2)) * 2 + apart // (feats // 2)
        return jnp.take(part, apart ^ feat_pos, axis=0).reshape(2, feats // 2, own, tokens)

    keep_early, send_early, keep_late, send_late = (blocks_of(part) for part in sums)
    everyone, low = (0, 1, 2, 3), (0, 1)

    def across_feat(x, bits, sections):
        pairs = [(s * feats + f, s * feats + (f ^ bits)) for s in sections for f in range(feats)]
        return lax.ppermute(x, ("section", "feat"), pairs)

    def halve(x, sections):
        return x[0] + across_feat(x[1].astype(BF16), 1, sections).astype(F32)

    def finish(x, sections):
        narrow = x.astype(BF16)
        total = x[0]
        for device in range(1, feats // 2):
            total = total + across_feat(narrow[device], 2 * device, sections).astype(F32)
        return total

    late = keep_late.astype(F32) + lax.ppermute(send_late, "section", [(0, 1), (1, 0), (2, 3)]).astype(F32)
    early = keep_early.astype(F32) + lax.ppermute(send_early, "section", [(0, 1)]).astype(F32)
    half = own // 2
    is_low = section_pos < 2
    crossed = lax.ppermute(late[:, :, :half].astype(BF16), "section", [(0, 2), (1, 3)]).astype(F32)
    second_late = finish(halve(late[:, :, half:], everyone), everyone)
    first = finish(halve(jnp.where(is_low, early[:, :, :half], late[:, :, :half] + crossed), everyone), everyone)
    second_early = finish(halve(early[:, :, half:], low), low)
    carried = lax.ppermute(second_late, "section", [(0, 2), (1, 3)])
    written = jnp.concatenate([first, jnp.where(is_low, second_early, second_late + carried)], axis=0)
    if relative:
        written = jnp.transpose(written.reshape(WIDE, tokens, LANES), (0, 2, 1)).reshape(own, tokens)
    return written.astype(BF16)[None]


def solution(mesh):
    in_specs = (
        P("section", None, None),
        P("section", None, "feat"),
        P("section", "feat", None, None),
        P("section", None, None),
    )
    out_specs = P("section", "feat", None)
    return jax.shard_map(local, mesh=mesh, in_specs=in_specs, out_specs=out_specs, check_vma=False)
```

```python
import functools

import jax
import jax.numpy as jnp
from jax import lax
from jax.experimental import pallas as pl
from jax.experimental.pallas import tpu as pltpu
from jax.sharding import PartitionSpec as P

LANES = 128
GROUP = 4
RING = 7
WIDE = 4
LEAD = 2
WINDOW = 5
F32 = jnp.float32
BF16 = jnp.bfloat16


def iota(shape, dim):
    return lax.broadcasted_iota(jnp.int32, shape, dim)


def dot(a, b):
    return jnp.dot(a, b, preferred_element_type=F32)


def dot_t(a, b):
    return lax.dot_general(a, b, (((1,), (1,)), ((), ())), preferred_element_type=F32)


def kernel(
    feats,
    relative,
    ids_hbm,
    res_hbm,
    enc_hbm,
    dec_hbm,
    keep_early,
    send_early,
    keep_late,
    send_late,
    ids_v,
    lo_v,
    sh_v,
    bits_v,
    rank_v,
    res_v,
    enc_v,
    list_v,
    list_s,
    acts_v,
    lhs_v,
    buf,
    acc,
    out_v,
    small_sem,
    enc_sem,
    dec_sem,
    out_sem,
):
    tokens, width = res_v.shape
    shard = acts_v.shape[1]
    slots = list_v.shape[1]
    rows_hi = shard // LANES
    max_blocks = slots // LANES
    ring = buf.shape[0]
    wides = acc.shape[1]
    section_pos, feat_pos = lax.axis_index("section"), lax.axis_index("feat")
    core = section_pos % 2

    ids_copy = pltpu.make_async_copy(ids_hbm, ids_v, small_sem.at[0])
    ids_copy.start()
    res_copy = pltpu.make_async_copy(res_hbm, res_v, small_sem.at[1])
    res_copy.start()
    chunk = min(4 * LANES, shard)
    chunks = shard // chunk

    def enc_copy(i):
        columns = pl.ds(i * chunk, chunk) if isinstance(i, int) else pl.ds(pl.multiple_of(i * chunk, chunk), chunk)
        return pltpu.make_async_copy(enc_hbm.at[:, columns], enc_v.at[i], enc_sem.at[i])

    early = (chunks + 1) // 2
    for i in range(early):
        enc_copy(i).start()

    ids_copy.wait()
    local = ids_v[...] - feat_pos * shard
    inside = (local >= 0) & (local < shard)
    lo_v[...] = jnp.where(inside, local & (LANES - 1), -1)
    sh_v[...] = jnp.where(inside, jnp.left_shift(1, (local >> 7) & 31), 0)
    lane_of = iota((LANES, tokens), 0)

    def gather_bits(k, bits):
        hit = lo_v[pl.ds(k, 1), :] == lane_of
        return bits | jnp.where(hit, sh_v[pl.ds(k, 1), :], 0)

    bits_t = lax.fori_loop(0, ids_v.shape[0], gather_bits, jnp.zeros((LANES, tokens), jnp.int32), unroll=8)
    bits = bits_t.T
    bits_v[...] = bits
    union = bits
    while union.shape[0] > 1:
        half = union.shape[0] // 2
        union = union[:half] | union[half:]

    rows = 16 * (-(-rows_hi // 16))
    hi_of = iota((rows, LANES), 0)
    flags = jnp.where(hi_of < rows_hi, jnp.right_shift(jnp.broadcast_to(union, (rows, LANES)), hi_of & 31) & 1, 0)
    flags_f = flags.astype(F32)
    upper = (iota((LANES, LANES), 0) <= iota((LANES, LANES), 1)).astype(F32).astype(BF16)
    inclusive = dot(flags_f.astype(BF16), upper)
    row_total = jnp.broadcast_to(jnp.sum(flags_f, axis=1, keepdims=True), (rows, LANES))
    below = (iota((rows, rows), 1) < iota((rows, rows), 0)).astype(F32).astype(BF16)
    row_start = dot(below, row_total.astype(BF16))
    row_end = row_start + row_total
    count = jnp.sum(flags_f).astype(jnp.int32)
    rank_v[...] = jnp.where(flags > 0, row_start + inclusive - 1.0, -1.0)

    slot = iota((rows, slots), 1).astype(F32)
    start_w = jnp.concatenate([row_start] * max_blocks, axis=1)
    end_w = jnp.concatenate([row_end] * max_blocks, axis=1)
    in_row = (start_w <= slot) & (slot < end_w)
    in_row_f = in_row.astype(F32)
    row_of = jnp.sum(in_row_f * iota((rows, slots), 0).astype(F32), axis=0, keepdims=True)
    place = jnp.sum(jnp.where(in_row, slot - start_w, 0.0), axis=0, keepdims=True)
    tall = jnp.concatenate([inclusive, jnp.zeros((LANES - rows, LANES), F32)], axis=0) if rows < LANES else inclusive
    prefix = dot(tall.T[:, :rows].astype(BF16), in_row_f.astype(BF16))
    lane_in = jnp.sum((prefix <= place).astype(F32), axis=0, keepdims=True)
    latent = row_of * float(LANES) + lane_in
    slot_row = iota((1, slots), 1)
    list_v[...] = jnp.where(slot_row < count, latent.astype(jnp.int32), slot_row)
    list_copy = pltpu.make_async_copy(list_v, list_s, small_sem.at[2])
    list_copy.start()
    blocks = jnp.maximum(1, (count + (LANES - 1)) // LANES)
    groups = (blocks + (GROUP - 1)) // GROUP

    def gather(place, base, i):
        pltpu.make_async_copy(
            dec_hbm.at[list_s[0, base + i]],
            buf.at[place, :, :, pl.ds(pl.multiple_of(2 * i, 2), 2), :],
            dec_sem.at[place],
        ).start()

    def issue(block, carry):
        place = lax.rem(block, ring)

        def row(i, carry):
            gather(place, block * LANES, i)
            return carry

        return lax.fori_loop(0, LANES, row, carry, unroll=True)

    def encode(i):
        enc_copy(i).wait()
        pre = dot(res_v[...], enc_v[i])
        for q in range(chunk // LANES):
            hi = i * (chunk // LANES) + q
            active = (jnp.right_shift(bits_v[...], hi) & 1) > 0
            piece = jnp.maximum(pre[:, q * LANES : (q + 1) * LANES], 0.0)
            acts_v[:, pl.ds(pl.multiple_of(hi * LANES, LANES), LANES)] = jnp.where(active, piece, 0.0).astype(BF16)

    def encode_step(i, carry):
        encode(i)
        return carry

    res_copy.wait()
    for i in range(early, chunks):
        enc_copy(i).start()
    first_blocks = jnp.minimum(blocks, ring)
    lead = jnp.minimum(blocks, LEAD)
    lax.fori_loop(0, early, encode_step, 0)
    list_copy.wait()
    lax.fori_loop(0, lead, issue, 0)
    lax.fori_loop(early, chunks, encode_step, 0)
    lax.fori_loop(lead, first_blocks, issue, 0)

    twice = ((iota((LANES, 2 * LANES), 1) >> 1) == iota((LANES, 2 * LANES), 0)).astype(F32).astype(BF16)
    parity = iota((tokens, 2 * LANES), 1) & 1
    window = min(WINDOW, rows_hi)

    def row_at(slot):
        return list_s[0, jnp.clip(slot, 0, jnp.maximum(count - 1, 0))] >> 7

    def compact(b, start, many):
        want = (iota((LANES, LANES), 0) + b * LANES).astype(F32)
        chosen = jnp.concatenate(
            [(rank_v[pl.ds(start + q, 1), :] == want).astype(F32).astype(BF16) for q in range(many)], axis=1
        )
        from_acts = acts_v[:, pl.ds(pl.multiple_of(start * LANES, LANES), many * LANES)]
        picked = dot_t(from_acts, chosen).astype(BF16)
        doubled = dot(picked, twice)
        lhs_v[b, :tokens, :] = jnp.where(parity == core, doubled, 0.0).astype(BF16)
        lhs_v[b, tokens:, :] = jnp.where(parity == core, 0.0, doubled).astype(BF16)

    def compact_wide(b, carry):
        compact(b, 0, rows_hi)
        return carry

    starts = [jnp.minimum(row_at(b * LANES), rows_hi - window) for b in range(ring)]
    narrow_fits = blocks >= ring
    for b in range(ring):
        narrow_fits = narrow_fits & (row_at(b * LANES + LANES - 1) < starts[b] + window)

    @pl.when(narrow_fits)
    def _():
        for b in range(ring):
            compact(b, starts[b], window)

    lax.fori_loop(jnp.where(narrow_fits, ring, 0), blocks, compact_wide, 0)

    outs = {(0, 0): keep_early, (0, 1): send_early, (1, 0): keep_late, (1, 1): send_late}

    def out_copy(pair, part, wide, dest):
        return pltpu.make_async_copy(out_v.at[pair, wide, part], outs[pair, part].at[dest], out_sem)

    def multiply(group, size, first, last):
        places = [lax.rem(group * GROUP + b, ring) for b in range(size)]
        for place in places:
            pltpu.make_async_copy(buf.at[place], buf.at[place], dec_sem.at[place]).wait()
        left = jnp.concatenate([lhs_v[group * GROUP + b] for b in range(size)], axis=1)
        for pair in (1, 0):

            def wide_step(wide, carry):
                right = jnp.concatenate(
                    [
                        jnp.concatenate([buf[place, wide * WIDE + q, pair] for q in range(WIDE)], axis=1)
                        for place in places
                    ],
                    axis=0,
                )
                total = dot(left, right)
                if not first:
                    total = total + acc[pair, wide]
                if last:
                    narrow = total.astype(BF16)
                    for part in range(2):
                        for q in range(WIDE):
                            out_v[pair, wide, part, q] = narrow[
                                part * tokens : (part + 1) * tokens, q * LANES : (q + 1) * LANES
                            ]
                else:
                    acc[pair, wide] = total
                return carry

            lax.fori_loop(0, wides, wide_step, 0, unroll=True)
            if last:
                for wide in range(wides):
                    if relative:
                        apart = jnp.bitwise_xor(wide, feat_pos)
                        dest = (apart & 1) * (feats // 2) + (apart >> 1)
                    else:
                        dest = wide
                    for part in range(2):
                        out_copy(pair, part, wide, dest).start()

    def each_group(group, carry):
        here = blocks - group * GROUP
        for first in (True, False):
            at = (group == 0) if first else (group > 0)
            if max_blocks > GROUP:

                @pl.when(at & (here > GROUP))
                def _():
                    multiply(group, GROUP, first, False)

            elif not first:
                continue
            for size in range(1, min(GROUP, max_blocks) + 1):

                @pl.when(at & (here == size))
                def _():
                    multiply(group, size, first, True)

        if max_blocks > ring:
            done = (group + 1) * GROUP
            lax.fori_loop(jnp.minimum(blocks, done - GROUP + ring), jnp.minimum(blocks, done + ring), issue, 0)

        return carry

    lax.fori_loop(0, groups, each_group, 0)
    for pair in range(2):
        for wide in range(wides):
            for part in range(2):
                out_copy(pair, part, wide, 0).wait()


def partial_sums(ids, residual, enc, dec, feats, relative):
    tokens, width = residual.shape
    shard = enc.shape[1]
    tiles = width // LANES
    wides = tiles // WIDE
    max_blocks = -(-shard // LANES)
    slots = max_blocks * LANES
    ring = min(RING, max_blocks)
    rows = 16 * (-(-max_blocks // 16))
    chunks = shard // min(4 * LANES, shard)
    return pl.pallas_call(
        functools.partial(kernel, feats, relative),
        out_shape=[jax.ShapeDtypeStruct((wides, WIDE, tokens, LANES), BF16)] * 4,
        in_specs=[pl.BlockSpec(memory_space=pl.ANY)] * 4,
        out_specs=[pl.BlockSpec(memory_space=pl.ANY)] * 4,
        scratch_shapes=[
            pltpu.VMEM(ids.shape, jnp.int32),
            pltpu.VMEM(ids.shape, jnp.int32),
            pltpu.VMEM(ids.shape, jnp.int32),
            pltpu.VMEM((tokens, LANES), jnp.int32),
            pltpu.VMEM((rows, LANES), F32),
            pltpu.VMEM((tokens, width), BF16),
            pltpu.VMEM((chunks, width, shard // chunks), BF16),
            pltpu.VMEM((1, slots), jnp.int32),
            pltpu.SMEM((1, slots), jnp.int32),
            pltpu.VMEM((tokens, shard), BF16),
            pltpu.VMEM((max_blocks, 2 * tokens, 2 * LANES), BF16),
            pltpu.VMEM((ring, tiles, 2, 2 * LANES, LANES), BF16),
            pltpu.VMEM((2, wides, 2 * tokens, WIDE * LANES), F32),
            pltpu.VMEM((2, wides, 2, WIDE, tokens, LANES), BF16),
            pltpu.SemaphoreType.DMA((3,)),
            pltpu.SemaphoreType.DMA((chunks,)),
            pltpu.SemaphoreType.DMA((ring,)),
            pltpu.SemaphoreType.DMA,
        ],
        compiler_params=pltpu.CompilerParams(vmem_limit_bytes=62 * 2**20),
        cost_estimate=pl.CostEstimate(
            flops=4 * tokens * width * shard, bytes_accessed=2 * width * shard * 3, transcendentals=0
        ),
    )(ids, residual, enc, dec)


def local(residual, enc_weight, dec_weight, latent_ids):
    feats = lax.axis_size("feat")
    section_pos = lax.axis_index("section")
    feat_pos = lax.axis_index("feat")
    tokens, width = residual.shape[1:]
    shard = enc_weight.shape[2]
    tiles = width // LANES
    own = width // feats
    relative = own == WIDE * LANES
    ids = latent_ids[0].T
    dec = dec_weight[0].reshape(shard, 2, 2, tiles, LANES).transpose(0, 3, 1, 2, 4)
    sums = partial_sums(ids, residual[0], enc_weight[0], dec, feats, relative)

    def blocks_of(part):
        if relative:
            return part.reshape(2, feats // 2, own, LANES)
        part = jnp.transpose(part, (0, 1, 3, 2)).reshape(feats, own, tokens)
        apart = jnp.arange(feats)
        apart = (apart % (feats // 2)) * 2 + apart // (feats // 2)
        return jnp.take(part, apart ^ feat_pos, axis=0).reshape(2, feats // 2, own, tokens)

    keep_early, send_early, keep_late, send_late = (blocks_of(part) for part in sums)
    everyone, low = (0, 1, 2, 3), (0, 1)

    def across_feat(x, bits, sections):
        pairs = [(s * feats + f, s * feats + (f ^ bits)) for s in sections for f in range(feats)]
        return lax.ppermute(x, ("section", "feat"), pairs)

    def halve(x, sections):
        return x[0] + across_feat(x[1].astype(BF16), 1, sections).astype(F32)

    def finish(x, sections):
        narrow = x.astype(BF16)
        total = x[0]
        for device in reversed(range(1, feats // 2)):
            total = total + across_feat(narrow[device], 2 * device, sections).astype(F32)
        return total

    late = keep_late.astype(F32) + lax.ppermute(send_late, "section", [(0, 1), (1, 0), (2, 3)]).astype(F32)
    early = keep_early.astype(F32) + lax.ppermute(send_early, "section", [(0, 1)]).astype(F32)
    half = own // 2
    is_low = section_pos < 2
    crossed = lax.ppermute(late[:, :, :half].astype(BF16), "section", [(0, 2), (1, 3)]).astype(F32)
    second = [halve(late[:, :, half:], everyone), halve(early[:, :, half:], low)]
    second = finish(jnp.concatenate(second, axis=1), everyone)
    second_late, second_early = second[:half], second[half:]
    first = finish(halve(jnp.where(is_low, early[:, :, :half], late[:, :, :half] + crossed), everyone), everyone)
    carried = lax.ppermute(second_late, "section", [(0, 2), (1, 3)])
    written = jnp.concatenate([first, jnp.where(is_low, second_early, second_late + carried)], axis=0)
    if relative:
        written = jnp.transpose(written.reshape(WIDE, tokens, LANES), (0, 2, 1)).reshape(own, tokens)
    return written.astype(BF16)[None]


def solution(mesh):
    in_specs = (
        P("section", None, None),
        P("section", None, "feat"),
        P("section", "feat", None, None),
        P("section", None, None),
    )
    out_specs = P("section", "feat", None)
    return jax.shard_map(local, mesh=mesh, in_specs=in_specs, out_specs=out_specs, check_vma=False)
```

```python
import functools

import jax
import jax.numpy as jnp
from jax import lax
from jax.experimental import pallas as pl
from jax.experimental.pallas import tpu as pltpu
from jax.sharding import PartitionSpec as P

LANES = 128
GROUP = 4
RING = 7
WIDE = 4
LEAD = 2
WINDOW = 5
F32 = jnp.float32
BF16 = jnp.bfloat16


def iota(shape, dim):
    return lax.broadcasted_iota(jnp.int32, shape, dim)


def dot(a, b):
    return jnp.dot(a, b, preferred_element_type=F32)


def dot_t(a, b):
    return lax.dot_general(a, b, (((1,), (1,)), ((), ())), preferred_element_type=F32)


def kernel(
    feats,
    relative,
    ids_hbm,
    res_hbm,
    enc_hbm,
    dec_hbm,
    keep_early,
    send_early,
    keep_late,
    send_late,
    ids_v,
    lo_v,
    sh_v,
    bits_v,
    rank_v,
    res_v,
    enc_v,
    list_v,
    list_s,
    acts_v,
    lhs_v,
    buf,
    acc,
    out_v,
    small_sem,
    enc_sem,
    dec_sem,
    out_sem,
):
    tokens, width = res_v.shape
    shard = acts_v.shape[1]
    slots = list_v.shape[1]
    rows_hi = shard // LANES
    max_blocks = slots // LANES
    ring = buf.shape[0]
    wides = acc.shape[1]
    section_pos, feat_pos = lax.axis_index("section"), lax.axis_index("feat")
    core = section_pos % 2

    ids_copy = pltpu.make_async_copy(ids_hbm, ids_v, small_sem.at[0])
    ids_copy.start()
    res_copy = pltpu.make_async_copy(res_hbm, res_v, small_sem.at[1])
    res_copy.start()
    chunk = min(4 * LANES, shard)
    chunks = shard // chunk

    def enc_copy(i):
        columns = pl.ds(i * chunk, chunk) if isinstance(i, int) else pl.ds(pl.multiple_of(i * chunk, chunk), chunk)
        return pltpu.make_async_copy(enc_hbm.at[:, columns], enc_v.at[i], enc_sem.at[i])

    early = (chunks + 1) // 2
    for i in range(early):
        enc_copy(i).start()

    ids_copy.wait()
    local = ids_v[...] - feat_pos * shard
    inside = (local >= 0) & (local < shard)
    lo_v[...] = jnp.where(inside, local & (LANES - 1), -1)
    sh_v[...] = jnp.where(inside, jnp.left_shift(1, (local >> 7) & 31), 0)
    lane_of = iota((LANES, tokens), 0)

    def gather_bits(k, bits):
        hit = lo_v[pl.ds(k, 1), :] == lane_of
        return bits | jnp.where(hit, sh_v[pl.ds(k, 1), :], 0)

    bits_t = lax.fori_loop(0, ids_v.shape[0], gather_bits, jnp.zeros((LANES, tokens), jnp.int32), unroll=8)
    bits = bits_t.T
    bits_v[...] = bits
    union = bits
    while union.shape[0] > 1:
        half = union.shape[0] // 2
        union = union[:half] | union[half:]

    rows = 16 * (-(-rows_hi // 16))
    hi_of = iota((rows, LANES), 0)
    flags = jnp.where(hi_of < rows_hi, jnp.right_shift(jnp.broadcast_to(union, (rows, LANES)), hi_of & 31) & 1, 0)
    flags_f = flags.astype(F32)
    upper = (iota((LANES, LANES), 0) <= iota((LANES, LANES), 1)).astype(F32).astype(BF16)
    inclusive = dot(flags_f.astype(BF16), upper)
    row_total = jnp.broadcast_to(jnp.sum(flags_f, axis=1, keepdims=True), (rows, LANES))
    below = (iota((rows, rows), 1) < iota((rows, rows), 0)).astype(F32).astype(BF16)
    row_start = dot(below, row_total.astype(BF16))
    row_end = row_start + row_total
    count = jnp.sum(flags_f).astype(jnp.int32)
    rank_v[...] = jnp.where(flags > 0, row_start + inclusive - 1.0, -1.0)

    slot = iota((rows, slots), 1).astype(F32)
    start_w = jnp.concatenate([row_start] * max_blocks, axis=1)
    end_w = jnp.concatenate([row_end] * max_blocks, axis=1)
    in_row = (start_w <= slot) & (slot < end_w)
    in_row_f = in_row.astype(F32)
    row_of = jnp.sum(in_row_f * iota((rows, slots), 0).astype(F32), axis=0, keepdims=True)
    place = jnp.sum(jnp.where(in_row, slot - start_w, 0.0), axis=0, keepdims=True)
    tall = jnp.concatenate([inclusive, jnp.zeros((LANES - rows, LANES), F32)], axis=0) if rows < LANES else inclusive
    prefix = dot(tall.T[:, :rows].astype(BF16), in_row_f.astype(BF16))
    lane_in = jnp.sum((prefix <= place).astype(F32), axis=0, keepdims=True)
    latent = row_of * float(LANES) + lane_in
    slot_row = iota((1, slots), 1)
    list_v[...] = jnp.where(slot_row < count, latent.astype(jnp.int32), slot_row)
    list_copy = pltpu.make_async_copy(list_v, list_s, small_sem.at[2])
    list_copy.start()
    blocks = jnp.maximum(1, (count + (LANES - 1)) // LANES)
    groups = (blocks + (GROUP - 1)) // GROUP

    def gather(place, base, i):
        pltpu.make_async_copy(
            dec_hbm.at[list_s[0, base + i]],
            buf.at[place, :, :, pl.ds(pl.multiple_of(2 * i, 2), 2), :],
            dec_sem.at[place],
        ).start()

    def issue(block, carry):
        place = lax.rem(block, ring)

        def row(i, carry):
            gather(place, block * LANES, i)
            return carry

        return lax.fori_loop(0, LANES, row, carry, unroll=True)

    def encode(i):
        enc_copy(i).wait()
        pre = dot(res_v[...], enc_v[i])
        for q in range(chunk // LANES):
            hi = i * (chunk // LANES) + q
            active = (jnp.right_shift(bits_v[...], hi) & 1) > 0
            piece = jnp.maximum(pre[:, q * LANES : (q + 1) * LANES], 0.0)
            acts_v[:, pl.ds(pl.multiple_of(hi * LANES, LANES), LANES)] = jnp.where(active, piece, 0.0).astype(BF16)

    def encode_step(i, carry):
        encode(i)
        return carry

    res_copy.wait()
    for i in range(early, chunks):
        enc_copy(i).start()
    first_blocks = jnp.minimum(blocks, ring)
    lead = jnp.minimum(blocks, LEAD)
    lax.fori_loop(0, early, encode_step, 0)
    list_copy.wait()
    lax.fori_loop(0, lead, issue, 0)
    lax.fori_loop(early, chunks, encode_step, 0)
    lax.fori_loop(lead, first_blocks, issue, 0)

    twice = ((iota((LANES, 2 * LANES), 1) >> 1) == iota((LANES, 2 * LANES), 0)).astype(F32).astype(BF16)
    parity = iota((tokens, 2 * LANES), 1) & 1
    window = min(WINDOW, rows_hi)

    def row_at(slot):
        return list_s[0, jnp.clip(slot, 0, jnp.maximum(count - 1, 0))] >> 7

    def compact(b, start, many):
        want = (iota((LANES, LANES), 0) + b * LANES).astype(F32)
        chosen = jnp.concatenate(
            [(rank_v[pl.ds(start + q, 1), :] == want).astype(F32).astype(BF16) for q in range(many)], axis=1
        )
        from_acts = acts_v[:, pl.ds(pl.multiple_of(start * LANES, LANES), many * LANES)]
        picked = dot_t(from_acts, chosen).astype(BF16)
        doubled = dot(picked, twice)
        lhs_v[b, :tokens, :] = jnp.where(parity == core, doubled, 0.0).astype(BF16)
        lhs_v[b, tokens:, :] = jnp.where(parity == core, 0.0, doubled).astype(BF16)

    def compact_wide(b, carry):
        compact(b, 0, rows_hi)
        return carry

    starts = [jnp.minimum(row_at(b * LANES), rows_hi - window) for b in range(ring)]
    narrow_fits = blocks >= ring
    for b in range(ring):
        narrow_fits = narrow_fits & (row_at(b * LANES + LANES - 1) < starts[b] + window)

    @pl.when(narrow_fits)
    def _():
        for b in range(ring):
            compact(b, starts[b], window)

    lax.fori_loop(jnp.where(narrow_fits, ring, 0), blocks, compact_wide, 0)

    outs = {(0, 0): keep_early, (0, 1): send_early, (1, 0): keep_late, (1, 1): send_late}

    def out_copy(pair, part, wide, dest):
        return pltpu.make_async_copy(out_v.at[pair, wide, part], outs[pair, part].at[dest], out_sem)

    def multiply(group, size, first, last):
        places = [lax.rem(group * GROUP + b, ring) for b in range(size)]
        for place in places:
            pltpu.make_async_copy(buf.at[place], buf.at[place], dec_sem.at[place]).wait()
        left = jnp.concatenate([lhs_v[group * GROUP + b] for b in range(size)], axis=1)
        for pair in (1, 0):

            def wide_step(wide, carry):
                right = jnp.concatenate(
                    [
                        jnp.concatenate([buf[place, wide * WIDE + q, pair] for q in range(WIDE)], axis=1)
                        for place in places
                    ],
                    axis=0,
                )
                total = dot(left, right)
                if not first:
                    total = total + acc[pair, wide]
                if last:
                    narrow = total.astype(BF16)
                    for part in range(2):
                        for q in range(WIDE):
                            out_v[pair, wide, part, q] = narrow[
                                part * tokens : (part + 1) * tokens, q * LANES : (q + 1) * LANES
                            ]
                else:
                    acc[pair, wide] = total
                return carry

            lax.fori_loop(0, wides, wide_step, 0, unroll=True)
            if last:
                for wide in range(wides):
                    if relative:
                        apart = jnp.bitwise_xor(wide, feat_pos)
                        dest = (apart & 1) * (feats // 2) + (apart >> 1)
                    else:
                        dest = wide
                    for part in range(2):
                        out_copy(pair, part, wide, dest).start()

    def each_group(group, carry):
        here = blocks - group * GROUP
        for first in (True, False):
            at = (group == 0) if first else (group > 0)
            if max_blocks > GROUP:

                @pl.when(at & (here > GROUP))
                def _():
                    multiply(group, GROUP, first, False)

            elif not first:
                continue
            for size in range(1, min(GROUP, max_blocks) + 1):

                @pl.when(at & (here == size))
                def _():
                    multiply(group, size, first, True)

        if max_blocks > ring:
            done = (group + 1) * GROUP
            lax.fori_loop(jnp.minimum(blocks, done - GROUP + ring), jnp.minimum(blocks, done + ring), issue, 0)

        return carry

    lax.fori_loop(0, groups, each_group, 0)
    for pair in range(2):
        for wide in range(wides):
            for part in range(2):
                out_copy(pair, part, wide, 0).wait()


def partial_sums(ids, residual, enc, dec, feats, relative):
    tokens, width = residual.shape
    shard = enc.shape[1]
    tiles = width // LANES
    wides = tiles // WIDE
    max_blocks = -(-shard // LANES)
    slots = max_blocks * LANES
    ring = min(RING, max_blocks)
    rows = 16 * (-(-max_blocks // 16))
    chunks = shard // min(4 * LANES, shard)
    return pl.pallas_call(
        functools.partial(kernel, feats, relative),
        out_shape=[jax.ShapeDtypeStruct((wides, WIDE, tokens, LANES), BF16)] * 4,
        in_specs=[pl.BlockSpec(memory_space=pl.ANY)] * 4,
        out_specs=[pl.BlockSpec(memory_space=pl.ANY)] * 4,
        scratch_shapes=[
            pltpu.VMEM(ids.shape, jnp.int32),
            pltpu.VMEM(ids.shape, jnp.int32),
            pltpu.VMEM(ids.shape, jnp.int32),
            pltpu.VMEM((tokens, LANES), jnp.int32),
            pltpu.VMEM((rows, LANES), F32),
            pltpu.VMEM((tokens, width), BF16),
            pltpu.VMEM((chunks, width, shard // chunks), BF16),
            pltpu.VMEM((1, slots), jnp.int32),
            pltpu.SMEM((1, slots), jnp.int32),
            pltpu.VMEM((tokens, shard), BF16),
            pltpu.VMEM((max_blocks, 2 * tokens, 2 * LANES), BF16),
            pltpu.VMEM((ring, tiles, 2, 2 * LANES, LANES), BF16),
            pltpu.VMEM((2, wides, 2 * tokens, WIDE * LANES), F32),
            pltpu.VMEM((2, wides, 2, WIDE, tokens, LANES), BF16),
            pltpu.SemaphoreType.DMA((3,)),
            pltpu.SemaphoreType.DMA((chunks,)),
            pltpu.SemaphoreType.DMA((ring,)),
            pltpu.SemaphoreType.DMA,
        ],
        compiler_params=pltpu.CompilerParams(vmem_limit_bytes=62 * 2**20),
        cost_estimate=pl.CostEstimate(
            flops=4 * tokens * width * shard, bytes_accessed=2 * width * shard * 3, transcendentals=0
        ),
    )(ids, residual, enc, dec)


def local(residual, enc_weight, dec_weight, latent_ids):
    feats = lax.axis_size("feat")
    section_pos = lax.axis_index("section")
    feat_pos = lax.axis_index("feat")
    tokens, width = residual.shape[1:]
    shard = enc_weight.shape[2]
    tiles = width // LANES
    own = width // feats
    relative = own == WIDE * LANES
    ids = latent_ids[0].T
    dec = dec_weight[0].reshape(shard, 2, 2, tiles, LANES).transpose(0, 3, 1, 2, 4)
    sums = partial_sums(ids, residual[0], enc_weight[0], dec, feats, relative)

    def blocks_of(part):
        if relative:
            return part.reshape(2, feats // 2, own, LANES)
        part = jnp.transpose(part, (0, 1, 3, 2)).reshape(feats, own, tokens)
        apart = jnp.arange(feats)
        apart = (apart % (feats // 2)) * 2 + apart // (feats // 2)
        return jnp.take(part, apart ^ feat_pos, axis=0).reshape(2, feats // 2, own, tokens)

    keep_early, send_early, keep_late, send_late = (blocks_of(part) for part in sums)
    everyone, low = (0, 1, 2, 3), (0, 1)

    def across_feat(x, bits, sections):
        pairs = [(s * feats + f, s * feats + (f ^ bits)) for s in sections for f in range(feats)]
        return lax.ppermute(x, ("section", "feat"), pairs)

    def halve(x, sections):
        return x[0] + across_feat(x[1].astype(BF16), 1, sections).astype(F32)

    def finish(x, sections):
        narrow = x.astype(BF16)
        total = x[0]
        for device in reversed(range(1, feats // 2)):
            total = total + across_feat(narrow[device], 2 * device, sections).astype(F32)
        return total

    late = keep_late.astype(F32) + lax.ppermute(send_late, "section", [(0, 1), (1, 0), (2, 3)]).astype(F32)
    early = keep_early.astype(F32) + lax.ppermute(send_early, "section", [(0, 1)]).astype(F32)
    half = own // 2
    is_low = section_pos < 2
    crossing = lax.optimization_barrier(late[:, :, :half].astype(BF16))
    crossed = lax.ppermute(crossing, "section", [(0, 2), (1, 3)]).astype(F32)
    second = [halve(late[:, :, half:], everyone), halve(early[:, :, half:], low)]
    second = finish(jnp.concatenate(second, axis=1), everyone)
    second_late, second_early = second[:half], second[half:]
    first = finish(halve(jnp.where(is_low, early[:, :, :half], crossing.astype(F32) + crossed), everyone), everyone)
    carried = lax.ppermute(second_late, "section", [(0, 2), (1, 3)])
    written = jnp.concatenate([first, jnp.where(is_low, second_early, second_late + carried)], axis=0)
    if relative:
        written = jnp.transpose(written.reshape(WIDE, tokens, LANES), (0, 2, 1)).reshape(own, tokens)
    return written.astype(BF16)[None]


def solution(mesh):
    in_specs = (
        P("section", None, None),
        P("section", None, "feat"),
        P("section", "feat", None, None),
        P("section", None, None),
    )
    out_specs = P("section", "feat", None)
    return jax.shard_map(local, mesh=mesh, in_specs=in_specs, out_specs=out_specs, check_vma=False)
```
